32 devices in a mesh: parts: 2 (over y), row: 4 (over x, core), col: 4 (over z).
Axes of the slice: x: 2, y: 2, z: 4, core: 2. Of those that a mesh axis runs over, the one named last changes fastest.
Arguments:
- tiles: bfloat16 [8, 4, 96, 128, 128], P(('parts', 'row'), 'col'), parts along dimension 0, may hold values from 0 to 6, as said below
- tile_rows: int32 [8, 4, 96], P(('parts', 'row'), 'col'), parts along dimension 0, may hold values from 0 to 63, as said below
- tile_cols: int32 [8, 4, 96], P(('parts', 'row'), 'col'), parts along dimension 0, may hold values from 0 to 63
- tile_counts: int32 [8, 4], P(('parts', 'row'), 'col'), parts along dimension 0, may hold values from 1 to 96, as said below
- seed_pages: int32 [16, 32], P('parts'), parts along dimension 0, may hold values from 0 to 32767, as said below
- seed_mass: float32 [16, 32], P('parts'), parts along dimension 0, may hold values from 4 to 32
- heat_time: float32 [16], P('parts'), parts along dimension 0, may hold values from 1 to 4
Outputs:
- heat: float32 [512, 8, 128], P(('parts', 'row', 'col')), parts along dimension 0
The draws below stay inside these ranges and needn't reach their ends.
There are 2 independent parts, one for each index of `parts`. The reference program is written for one: setup_inputs(seed, part) draws one part's arguments, and reference() takes and returns one part's arrays. A program takes and returns all parts, laid end to end along the dimension named above; each array names one. Nothing has to cross between parts.
Inputs may be any that keep to these rules, and one draw needn't show every extreme that they name: `tile_counts`: at least one device holds exactly 96 used slots. The pairs (tile_rows, tile_cols) of one device's 96 slots are all distinct. `tiles`: entries are zero or positive. `seed_pages`: seed k of every set lies in piece number k mod 16 (pieces numbered r * 4 + c).
All inputs are finite; a program needn't handle non-finite values.
Results may differ from the reference program's by a relative error of at most 0.005.
Values may be sent and summed in bfloat16 or wider, within the bound.
A program may use at most 64 MiB of HBM per device.

```python
import math
import jax
import jax.numpy as jnp
from jax import lax

SETS = 8
PB = 16
MAXT = 96
K_TERMS = 3
NBLK = 256
PAGES = 32768
SEEDK = 32
N_ROW = 4
N_COL = 4


def slot_pairs(key):
    keys = jax.random.split(key, N_ROW * N_COL)
    picks = jax.vmap(lambda k: jax.random.permutation(k, PB * N_COL * PB * N_ROW)[:MAXT])(keys)
    return picks.reshape(N_ROW, N_COL, MAXT).astype(jnp.int32)


def draw_tile_rows(key, part):
    picks = slot_pairs(key)
    return (picks // (PB * N_ROW)).astype(jnp.int32)


def draw_tile_cols(key, part):
    picks = slot_pairs(key)
    return (picks % (PB * N_ROW)).astype(jnp.int32)


def draw_tile_counts(key, part):
    key = jax.random.fold_in(key, 13)
    first, second, third = jax.random.split(key, 3)
    left = jax.random.randint(first, (N_ROW * N_COL,), 1, 5)
    right = jax.random.randint(second, (N_ROW * N_COL,), 1, 5)
    counts = jnp.maximum(1, MAXT * left * right // 16)
    chosen = jax.random.randint(third, (), 0, N_ROW * N_COL)
    counts = jnp.where(jnp.arange(N_ROW * N_COL) == chosen, MAXT, counts)
    return counts.reshape(N_ROW, N_COL).astype(jnp.int32)


def draw_tiles(key, part):
    key = jax.random.fold_in(key, 14)
    first, second = jax.random.split(key)
    shape = (N_ROW, N_COL, MAXT, 128, 128)
    present = jax.random.randint(first, shape, 0, 16) == 0
    weights = jnp.exp(jax.random.uniform(second, shape, jnp.float32, 0.0, math.log(4.0)))
    return jnp.where(present, weights, 0.0).astype(jnp.bfloat16)


def draw_seed_pages(key, part):
    key = jax.random.fold_in(key, 15)
    offsets = jax.random.randint(key, (SETS, SEEDK), 0, PB * 128)
    pieces = jnp.arange(SEEDK, dtype=jnp.int32) % (N_ROW * N_COL)
    return (pieces[None, :] * (PB * 128) + offsets).astype(jnp.int32)


def setup_inputs(seed: int = 0, part: int = 0) -> dict:
    seeds = jax.random.split(jax.random.key(seed), 8)
    own_keys = jax.random.split(jax.random.fold_in(seeds[7], part), 8)
    return {
        "tiles": draw_tiles(jax.random.fold_in(jax.random.fold_in(seeds[7], part), 71), part),
        "tile_rows": draw_tile_rows(jax.random.fold_in(jax.random.fold_in(seeds[7], part), 71), part),
        "tile_cols": draw_tile_cols(jax.random.fold_in(jax.random.fold_in(seeds[7], part), 71), part),
        "tile_counts": draw_tile_counts(jax.random.fold_in(jax.random.fold_in(seeds[7], part), 71), part),
        "seed_pages": draw_seed_pages(jax.random.fold_in(jax.random.fold_in(seeds[7], part), 71), part),
        "seed_mass": jnp.clip(jnp.exp(jax.random.uniform(own_keys[5], (SETS, SEEDK), jnp.float32, math.log(4.0), math.log(32.0))), 4.0, 32.0),
        "heat_time": jnp.clip(jnp.exp(jax.random.uniform(own_keys[6], (SETS,), jnp.float32, math.log(1.0), math.log(4.0))), 1.0, 4.0),
    }


def device_colsum(tile_set, cols, valid):
    sums = jnp.sum(tile_set.astype(jnp.float32), axis=1) * valid[:, None]
    return jax.ops.segment_sum(sums, cols, num_segments=PB * N_ROW)


def device_image(tile_set, rows, cols, valid, column_z):
    picked = jnp.take(column_z, cols, axis=0).astype(jnp.float32)
    prod = jnp.einsum("tsb,tab->tsa", picked, tile_set.astype(jnp.float32))
    prod = prod * valid[:, None, None]
    return jax.ops.segment_sum(prod, rows, num_segments=PB * N_COL)


def reference(tiles, tile_rows, tile_cols, tile_counts, seed_pages, seed_mass, heat_time):
    valid = (jnp.arange(MAXT)[None, None, :] < tile_counts[:, :, None]).astype(jnp.float32)
    colsums = lax.map(lambda r: jax.vmap(device_colsum)(tiles[r], tile_cols[r], valid[r]), jnp.arange(N_ROW))
    group_sums = jnp.sum(colsums, axis=0)
    degree = 1.0 + group_sums.reshape(N_COL, N_ROW, PB, 128).transpose(1, 0, 2, 3).reshape(NBLK, 128)
    flat_ids = (jnp.arange(SETS, dtype=jnp.int32)[:, None] * PAGES + seed_pages).reshape(-1)
    start = jax.ops.segment_sum(seed_mass.reshape(-1), flat_ids, num_segments=SETS * PAGES)
    value = start.reshape(SETS, NBLK, 128).transpose(1, 0, 2)
    total = value
    scale = heat_time[None, :, None]
    for step in range(K_TERMS):
        scaled = (value / degree[:, None, :]).astype(jnp.bfloat16)
        column_z = scaled.reshape(N_ROW, N_COL, PB, SETS, 128).transpose(1, 0, 2, 3, 4).reshape(N_COL, PB * N_ROW, SETS, 128)

        def row_group(r):
            parts_of_row = jax.vmap(device_image)(tiles[r], tile_rows[r], tile_cols[r], valid[r], column_z)
            return jnp.sum(parts_of_row, axis=0)

        image = lax.map(row_group, jnp.arange(N_ROW)).reshape(NBLK, SETS, 128)
        value = (scale / (step + 1.0)) * (image + scaled.astype(jnp.float32))
        total = total + value
    return jnp.exp(-scale) * total
```

```python
import functools

import jax
import jax.numpy as jnp
from jax import lax
from jax.experimental import pallas as pl
from jax.experimental.pallas import tpu as pltpu
from jax.sharding import PartitionSpec as P

PB = 16
K_TERMS = 3
LANES = 128
CHAINS = 2
MESH = pl.DeviceIdType.MESH


def kernel(
    n_row, n_col,
    tiles_hbm, rows_v, cols_v, cols_s, count_s, pages_v, mass_v, heat_s,
    out,
    tv, colsum, csend, crecv, degree, zf, zs, zr, chain0, chain1, ps, pr, idx_v, idx_s,
    tile_sem, idx_sem, c_send_sem, c_recv_sem, z_send_sem, z_recv_sem, p_send_sem, p_recv_sem,
):
    my_row = lax.axis_index("row")
    my_col = lax.axis_index("col")
    slots = tv.shape[0]
    sets = mass_v.shape[0]
    pieces = n_row * n_col
    chunks = tile_sem.shape[0]
    per_chunk = slots // chunks
    col_blocks = PB * n_row
    pairs = slots // 2

    def tile_copy(i):
        span = pl.ds(i * per_chunk, per_chunk)
        return pltpu.make_async_copy(tiles_hbm.at[0, 0, span], tv.at[span], tile_sem.at[i])

    for i in range(chunks):
        tile_copy(i).start()

    barrier = pltpu.get_barrier_semaphore()
    for d in range(1, n_row):
        pl.semaphore_signal(
            barrier, inc=1, device_id={"row": lax.rem(my_row + d, n_row)}, device_id_type=MESH
        )
    for d in range(1, n_col):
        pl.semaphore_signal(
            barrier, inc=1, device_id={"col": lax.rem(my_col + d, n_col)}, device_id_type=MESH
        )

    count = count_s[0, 0]
    rows_lane = rows_v[0]
    sub = lax.broadcasted_iota(jnp.int32, (slots, slots), 0)
    lane = lax.broadcasted_iota(jnp.int32, (slots, slots), 1)
    rows_sub = jnp.sum(
        jnp.where(sub == lane, jnp.broadcast_to(rows_lane, (slots, slots)), 0), axis=1, keepdims=True
    )
    same = (rows_sub == rows_lane) & (sub < lane) & ((sub & 1) == (lane & 1))
    idx_v[...] = jnp.zeros_like(idx_v)
    idx_v[0:1, 0:slots] = jnp.max(jnp.where(same, (sub >> 1) + 1, 0), axis=0, keepdims=True)
    wide = idx_v.shape[1]
    sub_w = lax.broadcasted_iota(jnp.int32, (slots, wide), 0)
    lane_w = lax.broadcasted_iota(jnp.int32, (slots, wide), 1)
    hit = (rows_sub == lane_w) & (sub_w < count)
    for p in range(CHAINS):
        found = jnp.where(hit & ((sub_w & 1) == p), (sub_w >> 1) + 1, 0)
        idx_v[1 + p : 2 + p, :] = jnp.max(found, axis=0, keepdims=True)
    idx_copy = pltpu.make_async_copy(idx_v, idx_s, idx_sem)
    idx_copy.start()

    def sum_chunk(i, carry):
        tile_copy(i).wait()
        for u in range(per_chunk // 8):
            span = pl.ds(pl.multiple_of(i * per_chunk + u * 8, 8), 8)
            colsum[span, :] = jnp.sum(tv[span].astype(jnp.float32), axis=1)
        return carry

    lax.fori_loop(0, chunks, sum_chunk, 0)
    block = lax.broadcasted_iota(jnp.int32, (col_blocks, slots), 0)
    slot = lax.broadcasted_iota(jnp.int32, (col_blocks, slots), 1)
    onehot = jnp.where((cols_v[0] == block) & (slot < count), 1.0, 0.0)
    csend[...] = jnp.dot(
        onehot, colsum[...], precision=lax.Precision.HIGHEST, preferred_element_type=jnp.float32
    )

    pl.semaphore_wait(barrier, n_row + n_col - 2)

    def c_copy(d):
        return pltpu.make_async_remote_copy(
            src_ref=csend, dst_ref=crecv.at[d - 1],
            send_sem=c_send_sem.at[d - 1], recv_sem=c_recv_sem.at[d - 1],
            device_id={"row": lax.rem(my_row + d, n_row)}, device_id_type=MESH,
        )

    for d in range(1, n_row):
        c_copy(d).start()

    set_id = lax.broadcasted_iota(jnp.int32, (sets, LANES), 0)
    page_lane = lax.broadcasted_iota(jnp.int32, (sets, LANES), 1)
    scale = jnp.zeros((sets, LANES), jnp.float32)
    for s in range(sets):
        scale = jnp.where(set_id == s, heat_s[s], scale)
    pages = pages_v[...]
    mass = mass_v[...]
    seeds = pages.shape[1]
    seed_lane = lax.broadcasted_iota(jnp.int32, pages.shape, 1)

    def seeds_of(piece):
        found = []
        for j in range(-(-seeds // pieces)):
            pick = seed_lane == piece + j * pieces
            offset = jnp.sum(jnp.where(pick, pages, 0), axis=1, keepdims=True) - piece * (PB * LANES)
            weight = jnp.sum(jnp.where(pick, mass, 0.0), axis=1, keepdims=True)
            found.append((offset - page_lane, jnp.broadcast_to(weight, (sets, LANES))))
        return found

    def seed_block(found, b):
        return sum(jnp.where(gap == b * LANES, weight, 0.0) for gap, weight in found)

    own = seeds_of(my_row * n_col + my_col)
    for b in range(PB):
        out[b] = seed_block(own, b)
    zero = jnp.zeros((sets, LANES), jnp.float32)
    chain0[0] = zero
    chain1[0] = zero

    idx_copy.wait()
    total = csend[...] + 1.0
    for d in range(1, n_row):
        c_copy(d).wait_recv()
        total = total + crecv[d - 1]
    degree[...] = total

    def seed_piece(r, carry):
        found = seeds_of(r * n_col + my_col)
        deg = degree[pl.ds(pl.multiple_of(r * PB, PB), PB), :]
        for b in range(PB):
            z = seed_block(found, b) / deg[b : b + 1, :]
            zf[r * PB + b] = z.astype(jnp.bfloat16).astype(jnp.float32)
        return carry

    lax.fori_loop(0, n_row, seed_piece, 0)

    def p_copy(k, d):
        return pltpu.make_async_remote_copy(
            src_ref=ps.at[k, d - 1], dst_ref=pr.at[k, d - 1],
            send_sem=p_send_sem.at[k, d - 1], recv_sem=p_recv_sem.at[k, d - 1],
            device_id={"col": lax.rem(my_col + d, n_col)}, device_id_type=MESH,
        )

    def z_copy(k, d):
        return pltpu.make_async_remote_copy(
            src_ref=zs.at[k], dst_ref=zr.at[k, d - 1],
            send_sem=z_send_sem.at[k, d - 1], recv_sem=z_recv_sem.at[k, d - 1],
            device_id={"row": lax.rem(my_row + d, n_row)}, device_id_type=MESH,
        )

    def row_sum(r):
        return chain0[idx_s[1, r]] + chain1[idx_s[2, r]]

    group = 12 if pairs % 12 == 0 else 1
    for k in range(K_TERMS):

        def multiply(g, carry):
            for u in range(group):
                j = g * group + u
                left = jnp.concatenate([zf[cols_s[0, 0, 2 * j]], zf[cols_s[0, 0, 2 * j + 1]]], axis=0)
                right = tv[pl.ds(2 * j, 2)].reshape(2 * LANES, LANES)
                prod = lax.dot_general(
                    left.astype(jnp.bfloat16), right, (((1,), (1,)), ((), ())),
                    preferred_element_type=jnp.float32,
                )
                chain0[j + 1] = prod[:sets, :LANES] + chain0[idx_s[0, 2 * j]]
                chain1[j + 1] = prod[sets:, LANES:] + chain1[idx_s[0, 2 * j + 1]]
            return carry

        lax.fori_loop(0, pairs // group, multiply, 0)

        def send_partial(d, carry):
            first = lax.rem(my_col + d, n_col) * PB
            for b in range(0, PB, 2):
                both = jnp.concatenate([row_sum(first + b), row_sum(first + b + 1)], axis=0)
                ps[k, d - 1, b * sets : (b + 2) * sets, :] = both.astype(jnp.bfloat16)
            p_copy(k, d).start()
            return carry

        lax.fori_loop(1, n_col, send_partial, 0)
        image = [row_sum(my_col * PB + b) + zf[my_row * PB + b] for b in range(PB)]
        for d in range(1, n_col):
            p_copy(k, d).wait_recv()
            for b in range(0, PB, 2):
                both = pr[k, d - 1, b * sets : (b + 2) * sets, :].astype(jnp.float32)
                image[b] = image[b] + both[:sets]
                image[b + 1] = image[b + 1] + both[sets:]
        factor = scale / (k + 1.0)
        value = [factor * x for x in image]
        if k == K_TERMS - 1:
            decay = jnp.exp(-scale)
            for b in range(PB):
                out[b] = decay * (out[b] + value[b])
            break
        deg = degree[pl.ds(pl.multiple_of(my_row * PB, PB), PB), :]
        for b in range(0, PB, 2):
            both = jnp.concatenate(
                [value[b] / deg[b : b + 1, :], value[b + 1] / deg[b + 1 : b + 2, :]], axis=0
            ).astype(jnp.bfloat16)
            zs[k, b * sets : (b + 2) * sets, :] = both
        for d in range(1, n_row):
            z_copy(k, d).start()

        def unpack(src, first):
            for b in range(0, PB, 2):
                both = src[b * sets : (b + 2) * sets, :].astype(jnp.float32)
                zf[first + b] = both[:sets]
                zf[first + b + 1] = both[sets:]

        unpack(zs.at[k], my_row * PB)
        for b in range(PB):
            out[b] = out[b] + value[b]
        for d in range(1, n_row):
            z_copy(k, d).wait_recv()
            unpack(zr.at[k, d - 1], lax.rem(my_row + n_row - d, n_row) * PB)

    for d in range(1, n_row):
        c_copy(d).wait_send()
        for k in range(K_TERMS - 1):
            z_copy(k, d).wait_send()
    for d in range(1, n_col):
        for k in range(K_TERMS):
            p_copy(k, d).wait_send()


def per_device(tiles, tile_rows, tile_cols, tile_counts, seed_pages, seed_mass, heat_time):
    n_row = lax.axis_size("row")
    n_col = lax.axis_size("col")
    slots = tiles.shape[2]
    sets = seed_mass.shape[0]
    chunks = 6 if slots % 48 == 0 else 1
    wide = max(LANES, PB * n_col)
    piece = (PB * sets, LANES)
    vmem = pl.BlockSpec(memory_space=pltpu.VMEM)
    smem = pl.BlockSpec(memory_space=pltpu.SMEM)
    dma = pltpu.SemaphoreType.DMA
    return pl.pallas_call(
        functools.partial(kernel, n_row, n_col),
        out_shape=jax.ShapeDtypeStruct((PB, sets, LANES), jnp.float32),
        in_specs=[pl.BlockSpec(memory_space=pl.ANY), vmem, vmem, smem, smem, vmem, vmem, smem],
        out_specs=vmem,
        scratch_shapes=[
            pltpu.VMEM((slots, LANES, LANES), jnp.bfloat16),
            pltpu.VMEM((slots, LANES), jnp.float32),
            pltpu.VMEM((PB * n_row, LANES), jnp.float32),
            pltpu.VMEM((n_row - 1, PB * n_row, LANES), jnp.float32),
            pltpu.VMEM((PB * n_row, LANES), jnp.float32),
            pltpu.VMEM((PB * n_row, sets, LANES), jnp.float32),
            pltpu.VMEM((K_TERMS - 1,) + piece, jnp.bfloat16),
            pltpu.VMEM((K_TERMS - 1, n_row - 1) + piece, jnp.bfloat16),
            pltpu.VMEM((slots // 2 + 1, sets, LANES), jnp.float32),
            pltpu.VMEM((slots // 2 + 1, sets, LANES), jnp.float32),
            pltpu.VMEM((K_TERMS, n_col - 1) + piece, jnp.bfloat16),
            pltpu.VMEM((K_TERMS, n_col - 1) + piece, jnp.bfloat16),
            pltpu.VMEM((8, wide), jnp.int32),
            pltpu.SMEM((8, wide), jnp.int32),
            dma((chunks,)),
            dma,
            dma((n_row - 1,)),
            dma((n_row - 1,)),
            dma((K_TERMS - 1, n_row - 1)),
            dma((K_TERMS - 1, n_row - 1)),
            dma((K_TERMS, n_col - 1)),
            dma((K_TERMS, n_col - 1)),
        ],
        compiler_params=pltpu.CompilerParams(
            collective_id=0, has_side_effects=True, vmem_limit_bytes=32 * 1024 * 1024
        ),
        name="heat_kernel",
    )(tiles, tile_rows, tile_cols, tile_cols, tile_counts, seed_pages, seed_mass, heat_time)


def solution(mesh):
    in_specs = (
        P(("parts", "row"), "col", None, None, None),
        P(("parts", "row"), "col", None),
        P(("parts", "row"), "col", None),
        P(("parts", "row"), "col"),
        P("parts", None),
        P("parts", None),
        P("parts"),
    )
    out_specs = P(("parts", "row", "col"), None, None)
    return jax.shard_map(
        per_device, mesh=mesh, in_specs=in_specs, out_specs=out_specs, check_vma=False
    )
```

```python
import functools

import jax
import jax.numpy as jnp
from jax import lax
from jax.experimental import pallas as pl
from jax.experimental.pallas import tpu as pltpu
from jax.sharding import PartitionSpec as P

PB = 16
K_TERMS = 3
LANES = 128
CHAINS = 2
MESH = pl.DeviceIdType.MESH


def kernel(
    n_row, n_col,
    tiles_hbm, rows_hbm, cols_hbm, count_hbm, pages_hbm, mass_hbm, heat_hbm,
    out,
    rows_v, cols_v, cols_s, count_s, pages_v, mass_v, heat_s, in_sem, tv, tt, colsum, csend, crecv, degree, zf, zs, zr, chain0, chain1, ps, pr, idx_v, idx_s,
    tile_sem, idx_sem, c_send_sem, c_recv_sem, z_send_sem, z_recv_sem, p_send_sem, p_recv_sem,
):
    my_row = lax.axis_index("row")
    my_col = lax.axis_index("col")
    slots = tv.shape[0]
    sets = mass_v.shape[0]
    pieces = n_row * n_col
    chunks = tile_sem.shape[0]
    per_chunk = slots // chunks
    col_blocks = PB * n_row
    pairs = slots // 2

    def tile_copy(i):
        span = pl.ds(i * per_chunk, per_chunk)
        return pltpu.make_async_copy(tiles_hbm.at[0, 0, span], tv.at[span], tile_sem.at[i])

    loads = [
        pltpu.make_async_copy(src, dst, in_sem.at[i])
        for i, (src, dst) in enumerate([
            (rows_hbm, rows_v), (count_hbm, count_s), (cols_hbm, cols_v), (cols_hbm, cols_s),
            (pages_hbm, pages_v), (mass_hbm, mass_v), (heat_hbm, heat_s),
        ])
    ]
    for load in loads:
        load.start()
    for i in range(chunks):
        tile_copy(i).start()

    near_last = sorted(range(1, n_row), key=lambda d: -min(d, n_row - d))

    barrier = pltpu.get_barrier_semaphore()
    for d in range(1, n_row):
        pl.semaphore_signal(
            barrier, inc=1, device_id={"row": lax.rem(my_row + d, n_row)}, device_id_type=MESH
        )
    for d in range(1, n_col):
        pl.semaphore_signal(
            barrier, inc=1, device_id={"col": lax.rem(my_col + d, n_col)}, device_id_type=MESH
        )

    for load in loads:
        load.wait()

    count = count_s[0, 0]

    def sum_chunk(i, carry):
        tile_copy(i).wait()
        for u in range(per_chunk // 8):
            span = pl.ds(pl.multiple_of(i * per_chunk + u * 8, 8), 8)
            colsum[span, :] = jnp.sum(tv[span].astype(jnp.float32), axis=1)
        return carry

    lax.fori_loop(0, chunks, sum_chunk, 0)
    block = lax.broadcasted_iota(jnp.int32, (col_blocks, slots), 0)
    slot = lax.broadcasted_iota(jnp.int32, (col_blocks, slots), 1)
    onehot = jnp.where((cols_v[0] == block) & (slot < count), 1.0, 0.0)
    csend[...] = jnp.dot(
        onehot, colsum[...], precision=lax.Precision.HIGHEST, preferred_element_type=jnp.float32
    )

    pl.semaphore_wait(barrier, n_row + n_col - 2)

    def c_copy(d):
        return pltpu.make_async_remote_copy(
            src_ref=csend, dst_ref=crecv.at[d - 1],
            send_sem=c_send_sem.at[d - 1], recv_sem=c_recv_sem.at[d - 1],
            device_id={"row": lax.rem(my_row + d, n_row)}, device_id_type=MESH,
        )

    for d in near_last:
        c_copy(d).start()

    turns = 8 if pairs % 8 == 0 else 1

    def turn(g, carry):
        for u in range(turns):
            j = g * turns + u
            tt[j, :, :LANES] = tv[2 * j].T
            tt[j, :, LANES:] = tv[2 * j + 1].T
        return carry

    lax.fori_loop(0, pairs // turns, turn, 0)

    rows_lane = rows_v[0]
    sub = lax.broadcasted_iota(jnp.int32, (slots, slots), 0)
    lane = lax.broadcasted_iota(jnp.int32, (slots, slots), 1)
    rows_sub = jnp.sum(
        jnp.where(sub == lane, jnp.broadcast_to(rows_lane, (slots, slots)), 0), axis=1, keepdims=True
    )
    same = (rows_sub == rows_lane) & (sub < lane) & ((sub & 1) == (lane & 1))
    idx_v[...] = jnp.zeros_like(idx_v)
    idx_v[0:1, 0:slots] = jnp.max(jnp.where(same, (sub >> 1) + 1, 0), axis=0, keepdims=True)
    wide = idx_v.shape[1]
    sub_w = lax.broadcasted_iota(jnp.int32, (slots, wide), 0)
    lane_w = lax.broadcasted_iota(jnp.int32, (slots, wide), 1)
    hit = (rows_sub == lane_w) & (sub_w < count)
    for p in range(CHAINS):
        found = jnp.where(hit & ((sub_w & 1) == p), (sub_w >> 1) + 1, 0)
        idx_v[1 + p : 2 + p, :] = jnp.max(found, axis=0, keepdims=True)
    idx_copy = pltpu.make_async_copy(idx_v, idx_s, idx_sem)
    idx_copy.start()

    set_id = lax.broadcasted_iota(jnp.int32, (sets, LANES), 0)
    page_lane = lax.broadcasted_iota(jnp.int32, (sets, LANES), 1)
    scale = jnp.zeros((sets, LANES), jnp.float32)
    for s in range(sets):
        scale = jnp.where(set_id == s, heat_s[s], scale)
    pages = pages_v[...]
    mass = mass_v[...]
    seeds = pages.shape[1]
    seed_lane = lax.broadcasted_iota(jnp.int32, pages.shape, 1)

    def seeds_of(piece):
        found = []
        for j in range(-(-seeds // pieces)):
            pick = seed_lane == piece + j * pieces
            offset = jnp.sum(jnp.where(pick, pages, 0), axis=1, keepdims=True) - piece * (PB * LANES)
            weight = jnp.sum(jnp.where(pick, mass, 0.0), axis=1, keepdims=True)
            found.append((offset - page_lane, jnp.broadcast_to(weight, (sets, LANES))))
        return found

    def seed_block(found, b):
        return sum(jnp.where(gap == b * LANES, weight, 0.0) for gap, weight in found)

    own = seeds_of(my_row * n_col + my_col)
    for b in range(PB):
        out[b] = seed_block(own, b)
    zero = jnp.zeros((sets, LANES), jnp.float32)
    chain0[0] = zero
    chain1[0] = zero

    idx_copy.wait()
    total = csend[...] + 1.0
    for d in range(1, n_row):
        c_copy(d).wait_recv()
        total = total + crecv[d - 1]
    degree[...] = total

    def seed_piece(r, carry):
        found = seeds_of(r * n_col + my_col)
        deg = degree[pl.ds(pl.multiple_of(r * PB, PB), PB), :]
        for b in range(PB):
            z = seed_block(found, b) / deg[b : b + 1, :]
            zf[r * PB + b] = z.astype(jnp.bfloat16).astype(jnp.float32)
        return carry

    lax.fori_loop(0, n_row, seed_piece, 0)

    def p_copy(k, d):
        return pltpu.make_async_remote_copy(
            src_ref=ps.at[k, d - 1], dst_ref=pr.at[k, d - 1],
            send_sem=p_send_sem.at[k, d - 1], recv_sem=p_recv_sem.at[k, d - 1],
            device_id={"col": lax.rem(my_col + d, n_col)}, device_id_type=MESH,
        )

    def z_copy(k, d):
        return pltpu.make_async_remote_copy(
            src_ref=zs.at[k], dst_ref=zr.at[k, d - 1],
            send_sem=z_send_sem.at[k, d - 1], recv_sem=z_recv_sem.at[k, d - 1],
            device_id={"row": lax.rem(my_row + d, n_row)}, device_id_type=MESH,
        )

    def row_sum(r):
        return chain0[idx_s[1, r]] + chain1[idx_s[2, r]]

    group = 48 if pairs % 48 == 0 else 1
    for k in range(K_TERMS):

        def multiply(g, carry):
            for u in range(group):
                j = g * group + u
                left = jnp.concatenate([zf[cols_s[0, 0, 2 * j]], zf[cols_s[0, 0, 2 * j + 1]]], axis=0)
                prod = lax.dot_general(
                    left.astype(jnp.bfloat16), tt[j], (((1,), (0,)), ((), ())),
                    preferred_element_type=jnp.float32,
                )
                chain0[j + 1] = prod[:sets, :LANES] + chain0[idx_s[0, 2 * j]]
                chain1[j + 1] = prod[sets:, LANES:] + chain1[idx_s[0, 2 * j + 1]]
            return carry

        lax.fori_loop(0, pairs // group, multiply, 0)

        def send_partial(d, carry):
            first = lax.rem(my_col + d, n_col) * PB
            for b in range(0, PB, 2):
                both = jnp.concatenate([row_sum(first + b), row_sum(first + b + 1)], axis=0)
                ps[k, d - 1, b * sets : (b + 2) * sets, :] = both.astype(jnp.bfloat16)
            p_copy(k, d).start()
            return carry

        lax.fori_loop(1, n_col, send_partial, 0)
        image = [row_sum(my_col * PB + b) + zf[my_row * PB + b] for b in range(PB)]
        for d in range(1, n_col):
            p_copy(k, d).wait_recv()
            for b in range(0, PB, 2):
                both = pr[k, d - 1, b * sets : (b + 2) * sets, :].astype(jnp.float32)
                image[b] = image[b] + both[:sets]
                image[b + 1] = image[b + 1] + both[sets:]
        factor = scale / (k + 1.0)
        value = [factor * x for x in image]
        if k == K_TERMS - 1:
            decay = jnp.exp(-scale)
            for b in range(PB):
                out[b] = decay * (out[b] + value[b])
            break
        deg = degree[pl.ds(pl.multiple_of(my_row * PB, PB), PB), :]
        for b in range(0, PB, 2):
            both = jnp.concatenate(
                [value[b] / deg[b : b + 1, :], value[b + 1] / deg[b + 1 : b + 2, :]], axis=0
            ).astype(jnp.bfloat16)
            zs[k, b * sets : (b + 2) * sets, :] = both
        for d in near_last:
            z_copy(k, d).start()

        def unpack(src, first):
            for b in range(0, PB, 2):
                both = src[b * sets : (b + 2) * sets, :].astype(jnp.float32)
                zf[first + b] = both[:sets]
                zf[first + b + 1] = both[sets:]

        unpack(zs.at[k], my_row * PB)
        for b in range(PB):
            out[b] = out[b] + value[b]
        for d in range(1, n_row):
            z_copy(k, d).wait_recv()
            unpack(zr.at[k, d - 1], lax.rem(my_row + n_row - d, n_row) * PB)

    for d in range(1, n_row):
        c_copy(d).wait_send()
        for k in range(K_TERMS - 1):
            z_copy(k, d).wait_send()
    for d in range(1, n_col):
        for k in range(K_TERMS):
            p_copy(k, d).wait_send()


def per_device(tiles, tile_rows, tile_cols, tile_counts, seed_pages, seed_mass, heat_time):
    n_row = lax.axis_size("row")
    n_col = lax.axis_size("col")
    slots = tiles.shape[2]
    sets = seed_mass.shape[0]
    chunks = 6 if slots % 48 == 0 else 1
    wide = max(LANES, PB * n_col)
    piece = (PB * sets, LANES)
    dma = pltpu.SemaphoreType.DMA
    return pl.pallas_call(
        functools.partial(kernel, n_row, n_col),
        out_shape=jax.ShapeDtypeStruct((PB, sets, LANES), jnp.float32),
        in_specs=[pl.BlockSpec(memory_space=pltpu.HBM)] * 7,
        out_specs=pl.BlockSpec(memory_space=pltpu.VMEM),
        scratch_shapes=[
            pltpu.VMEM(tile_rows.shape, jnp.int32),
            pltpu.VMEM(tile_cols.shape, jnp.int32),
            pltpu.SMEM(tile_cols.shape, jnp.int32),
            pltpu.SMEM(tile_counts.shape, jnp.int32),
            pltpu.VMEM(seed_pages.shape, jnp.int32),
            pltpu.VMEM(seed_mass.shape, jnp.float32),
            pltpu.SMEM(heat_time.shape, jnp.float32),
            dma((7,)),
            pltpu.VMEM((slots, LANES, LANES), jnp.bfloat16),
            pltpu.VMEM((slots // 2, LANES, 2 * LANES), jnp.bfloat16),
            pltpu.VMEM((slots, LANES), jnp.float32),
            pltpu.VMEM((PB * n_row, LANES), jnp.float32),
            pltpu.VMEM((n_row - 1, PB * n_row, LANES), jnp.float32),
            pltpu.VMEM((PB * n_row, LANES), jnp.float32),
            pltpu.VMEM((PB * n_row, sets, LANES), jnp.float32),
            pltpu.VMEM((K_TERMS - 1,) + piece, jnp.bfloat16),
            pltpu.VMEM((K_TERMS - 1, n_row - 1) + piece, jnp.bfloat16),
            pltpu.VMEM((slots // 2 + 1, sets, LANES), jnp.float32),
            pltpu.VMEM((slots // 2 + 1, sets, LANES), jnp.float32),
            pltpu.VMEM((K_TERMS, n_col - 1) + piece, jnp.bfloat16),
            pltpu.VMEM((K_TERMS, n_col - 1) + piece, jnp.bfloat16),
            pltpu.VMEM((8, wide), jnp.int32),
            pltpu.SMEM((8, wide), jnp.int32),
            dma((chunks,)),
            dma,
            dma((n_row - 1,)),
            dma((n_row - 1,)),
            dma((K_TERMS - 1, n_row - 1)),
            dma((K_TERMS - 1, n_row - 1)),
            dma((K_TERMS, n_col - 1)),
            dma((K_TERMS, n_col - 1)),
        ],
        compiler_params=pltpu.CompilerParams(
            collective_id=0, has_side_effects=True, vmem_limit_bytes=60 * 1024 * 1024
        ),
        name="heat_kernel",
    )(tiles, tile_rows, tile_cols, tile_counts, seed_pages, seed_mass, heat_time)


def solution(mesh):
    in_specs = (
        P(("parts", "row"), "col", None, None, None),
        P(("parts", "row"), "col", None),
        P(("parts", "row"), "col", None),
        P(("parts", "row"), "col"),
        P("parts", None),
        P("parts", None),
        P("parts"),
    )
    out_specs = P(("parts", "row", "col"), None, None)
    return jax.shard_map(
        per_device, mesh=mesh, in_specs=in_specs, out_specs=out_specs, check_vma=False
    )
```

```python
import functools

import jax
import jax.numpy as jnp
from jax import lax
from jax.experimental import pallas as pl
from jax.experimental.pallas import tpu as pltpu
from jax.sharding import PartitionSpec as P

PB = 16
K_TERMS = 3
LANES = 128
CHAINS = 2
MESH = pl.DeviceIdType.MESH


def kernel(
    n_row, n_col,
    tiles_hbm, rows_hbm, cols_hbm, count_hbm, pages_hbm, mass_hbm, heat_hbm,
    out_hbm,
    out, out_sem, rows_v, cols_v, cols_s, count_s, pages_v, mass_v, heat_s, in_sem, tv, tt, colsum, csend, crecv, degree, zf, zs, zr, chain0, chain1, ps, pr, idx_v, idx_s,
    tile_sem, idx_sem, c_send_sem, c_recv_sem, z_send_sem, z_recv_sem, p_send_sem, p_recv_sem,
):
    my_row = lax.axis_index("row")
    my_col = lax.axis_index("col")
    slots = tv.shape[0]
    sets = mass_v.shape[0]
    pieces = n_row * n_col
    chunks = tile_sem.shape[0]
    per_chunk = slots // chunks
    col_blocks = PB * n_row
    pairs = slots // 2

    def tile_copy(i):
        span = pl.ds(i * per_chunk, per_chunk)
        return pltpu.make_async_copy(tiles_hbm.at[0, 0, span], tv.at[span], tile_sem.at[i])

    near_last = sorted(range(1, n_row), key=lambda d: -min(d, n_row - d))

    barrier = pltpu.get_barrier_semaphore()
    for d in range(1, n_col):
        pl.semaphore_signal(
            barrier, inc=1, device_id={"col": lax.rem(my_col + d, n_col)}, device_id_type=MESH
        )
    for d in range(1, n_row):
        pl.semaphore_signal(
            barrier, inc=1, device_id={"row": lax.rem(my_row + d, n_row)}, device_id_type=MESH
        )

    for i in range(chunks):
        tile_copy(i).start()
    loads = [
        pltpu.make_async_copy(src, dst, in_sem.at[i])
        for i, (src, dst) in enumerate([
            (rows_hbm, rows_v), (count_hbm, count_s), (cols_hbm, cols_v), (cols_hbm, cols_s),
            (pages_hbm, pages_v), (mass_hbm, mass_v), (heat_hbm, heat_s),
        ])
    ]
    for load in loads:
        load.start()

    for load in loads:
        load.wait()

    count = count_s[0, 0]

    def sum_chunk(i, carry):
        tile_copy(i).wait()
        for u in range(per_chunk // 8):
            span = pl.ds(pl.multiple_of(i * per_chunk + u * 8, 8), 8)
            colsum[span, :] = jnp.sum(tv[span].astype(jnp.float32), axis=1)
        return carry

    lax.fori_loop(0, chunks, sum_chunk, 0)
    block = lax.broadcasted_iota(jnp.int32, (col_blocks, slots), 0)
    slot = lax.broadcasted_iota(jnp.int32, (col_blocks, slots), 1)
    onehot = jnp.where((cols_v[0] == block) & (slot < count), 1.0, 0.0)
    csend[...] = jnp.dot(
        onehot, colsum[...], precision=lax.Precision.HIGHEST, preferred_element_type=jnp.float32
    )

    pl.semaphore_wait(barrier, n_row + n_col - 2)

    def c_copy(d):
        return pltpu.make_async_remote_copy(
            src_ref=csend, dst_ref=crecv.at[d - 1],
            send_sem=c_send_sem.at[d - 1], recv_sem=c_recv_sem.at[d - 1],
            device_id={"row": lax.rem(my_row + d, n_row)}, device_id_type=MESH,
        )

    for d in near_last:
        c_copy(d).start()

    rows_lane = rows_v[0]
    sub = lax.broadcasted_iota(jnp.int32, (slots, slots), 0)
    lane = lax.broadcasted_iota(jnp.int32, (slots, slots), 1)
    rows_sub = jnp.sum(
        jnp.where(sub == lane, jnp.broadcast_to(rows_lane, (slots, slots)), 0), axis=1, keepdims=True
    )
    same = (rows_sub == rows_lane) & (sub < lane) & ((sub & 1) == (lane & 1))
    idx_v[...] = jnp.zeros_like(idx_v)
    idx_v[0:1, 0:slots] = jnp.max(jnp.where(same, (sub >> 1) + 1, 0), axis=0, keepdims=True)
    wide = idx_v.shape[1]
    sub_w = lax.broadcasted_iota(jnp.int32, (slots, wide), 0)
    lane_w = lax.broadcasted_iota(jnp.int32, (slots, wide), 1)
    hit = (rows_sub == lane_w) & (sub_w < count)
    for p in range(CHAINS):
        found = jnp.where(hit & ((sub_w & 1) == p), (sub_w >> 1) + 1, 0)
        idx_v[1 + p : 2 + p, :] = jnp.max(found, axis=0, keepdims=True)
    idx_copy = pltpu.make_async_copy(idx_v, idx_s, idx_sem)
    idx_copy.start()

    turns = 8 if pairs % 8 == 0 else 1

    def turn(g, carry):
        for u in range(turns):
            j = g * turns + u
            tt[j, :, :LANES] = tv[2 * j].T
            tt[j, :, LANES:] = tv[2 * j + 1].T
        return carry

    lax.fori_loop(0, pairs // turns, turn, 0)

    set_id = lax.broadcasted_iota(jnp.int32, (sets, LANES), 0)
    page_lane = lax.broadcasted_iota(jnp.int32, (sets, LANES), 1)
    scale = jnp.zeros((sets, LANES), jnp.float32)
    for s in range(sets):
        scale = jnp.where(set_id == s, heat_s[s], scale)
    pages = pages_v[...]
    mass = mass_v[...]
    seeds = pages.shape[1]
    seed_lane = lax.broadcasted_iota(jnp.int32, pages.shape, 1)

    def seeds_of(piece):
        found = []
        for j in range(-(-seeds // pieces)):
            pick = seed_lane == piece + j * pieces
            offset = jnp.sum(jnp.where(pick, pages, 0), axis=1, keepdims=True) - piece * (PB * LANES)
            weight = jnp.sum(jnp.where(pick, mass, 0.0), axis=1, keepdims=True)
            found.append((offset - page_lane, jnp.broadcast_to(weight, (sets, LANES))))
        return found

    def seed_block(found, b):
        return sum(jnp.where(gap == b * LANES, weight, 0.0) for gap, weight in found)

    own = seeds_of(my_row * n_col + my_col)
    for b in range(PB):
        out[b] = seed_block(own, b)
    zero = jnp.zeros((sets, LANES), jnp.float32)
    chain0[0] = zero
    chain1[0] = zero

    idx_copy.wait()
    total = csend[...] + 1.0
    for d in range(1, n_row):
        c_copy(d).wait_recv()
        total = total + crecv[d - 1]
    degree[...] = total

    def seed_piece(r, carry):
        found = seeds_of(r * n_col + my_col)
        deg = degree[pl.ds(pl.multiple_of(r * PB, PB), PB), :]
        for b in range(PB):
            z = seed_block(found, b) / deg[b : b + 1, :]
            zf[r * PB + b] = z.astype(jnp.bfloat16).astype(jnp.float32)
        return carry

    lax.fori_loop(0, n_row, seed_piece, 0)

    def p_copy(k, d):
        return pltpu.make_async_remote_copy(
            src_ref=ps.at[k, d - 1], dst_ref=pr.at[k, d - 1],
            send_sem=p_send_sem.at[k, d - 1], recv_sem=p_recv_sem.at[k, d - 1],
            device_id={"col": lax.rem(my_col + d, n_col)}, device_id_type=MESH,
        )

    def z_copy(k, d):
        return pltpu.make_async_remote_copy(
            src_ref=zs.at[k], dst_ref=zr.at[k, d - 1],
            send_sem=z_send_sem.at[k, d - 1], recv_sem=z_recv_sem.at[k, d - 1],
            device_id={"row": lax.rem(my_row + d, n_row)}, device_id_type=MESH,
        )

    quarter = PB // 4

    def out_copy(i):
        span = pl.ds(i * quarter, quarter)
        return pltpu.make_async_copy(out.at[span], out_hbm.at[span], out_sem.at[i])

    def row_sum(r):
        return chain0[idx_s[1, r]] + chain1[idx_s[2, r]]

    group = 48 if pairs % 48 == 0 else 1
    for k in range(K_TERMS):

        def multiply(g, carry):
            for u in range(group):
                j = g * group + u
                left = jnp.concatenate([zf[cols_s[0, 0, 2 * j]], zf[cols_s[0, 0, 2 * j + 1]]], axis=0)
                prod = lax.dot_general(
                    left.astype(jnp.bfloat16), tt[j], (((1,), (0,)), ((), ())),
                    preferred_element_type=jnp.float32,
                )
                chain0[j + 1] = prod[:sets, :LANES] + chain0[idx_s[0, 2 * j]]
                chain1[j + 1] = prod[sets:, LANES:] + chain1[idx_s[0, 2 * j + 1]]
            return carry

        lax.fori_loop(0, pairs // group, multiply, 0)

        def send_partial(d, carry):
            first = lax.rem(my_col + d, n_col) * PB
            for b in range(0, PB, 2):
                both = jnp.concatenate([row_sum(first + b), row_sum(first + b + 1)], axis=0)
                ps[k, d - 1, b * sets : (b + 2) * sets, :] = both.astype(jnp.bfloat16)
            p_copy(k, d).start()
            return carry

        lax.fori_loop(1, n_col, send_partial, 0)
        image = [row_sum(my_col * PB + b) + zf[my_row * PB + b] for b in range(PB)]
        for d in range(1, n_col):
            p_copy(k, d).wait_recv()
            for b in range(0, PB, 2):
                both = pr[k, d - 1, b * sets : (b + 2) * sets, :].astype(jnp.float32)
                image[b] = image[b] + both[:sets]
                image[b + 1] = image[b + 1] + both[sets:]
        factor = scale / (k + 1.0)
        value = [factor * x for x in image]
        if k == K_TERMS - 1:
            decay = jnp.exp(-scale)
            for b in range(PB):
                out[b] = decay * (out[b] + value[b])
                if b % quarter == quarter - 1:
                    out_copy(b // quarter).start()
            break
        deg = degree[pl.ds(pl.multiple_of(my_row * PB, PB), PB), :]
        for b in range(0, PB, 2):
            both = jnp.concatenate(
                [value[b] / deg[b : b + 1, :], value[b + 1] / deg[b + 1 : b + 2, :]], axis=0
            ).astype(jnp.bfloat16)
            zs[k, b * sets : (b + 2) * sets, :] = both
        for d in near_last:
            z_copy(k, d).start()

        def unpack(src, first):
            for b in range(0, PB, 2):
                both = src[b * sets : (b + 2) * sets, :].astype(jnp.float32)
                zf[first + b] = both[:sets]
                zf[first + b + 1] = both[sets:]

        unpack(zs.at[k], my_row * PB)
        for b in range(PB):
            out[b] = out[b] + value[b]
        for d in range(1, n_row):
            z_copy(k, d).wait_recv()
            unpack(zr.at[k, d - 1], lax.rem(my_row + n_row - d, n_row) * PB)

    for d in range(1, n_row):
        c_copy(d).wait_send()
        for k in range(K_TERMS - 1):
            z_copy(k, d).wait_send()
    for d in range(1, n_col):
        for k in range(K_TERMS):
            p_copy(k, d).wait_send()
    for i in range(4):
        out_copy(i).wait()


def per_device(tiles, tile_rows, tile_cols, tile_counts, seed_pages, seed_mass, heat_time):
    n_row = lax.axis_size("row")
    n_col = lax.axis_size("col")
    slots = tiles.shape[2]
    sets = seed_mass.shape[0]
    chunks = 6 if slots % 48 == 0 else 1
    wide = max(LANES, PB * n_col)
    piece = (PB * sets, LANES)
    dma = pltpu.SemaphoreType.DMA
    return pl.pallas_call(
        functools.partial(kernel, n_row, n_col),
        out_shape=jax.ShapeDtypeStruct((PB, sets, LANES), jnp.float32),
        in_specs=[pl.BlockSpec(memory_space=pltpu.HBM)] * 7,
        out_specs=pl.BlockSpec(memory_space=pltpu.HBM),
        scratch_shapes=[
            pltpu.VMEM((PB, sets, LANES), jnp.float32),
            dma((4,)),
            pltpu.VMEM(tile_rows.shape, jnp.int32),
            pltpu.VMEM(tile_cols.shape, jnp.int32),
            pltpu.SMEM(tile_cols.shape, jnp.int32),
            pltpu.SMEM(tile_counts.shape, jnp.int32),
            pltpu.VMEM(seed_pages.shape, jnp.int32),
            pltpu.VMEM(seed_mass.shape, jnp.float32),
            pltpu.SMEM(heat_time.shape, jnp.float32),
            dma((7,)),
            pltpu.VMEM((slots, LANES, LANES), jnp.bfloat16),
            pltpu.VMEM((slots // 2, LANES, 2 * LANES), jnp.bfloat16),
            pltpu.VMEM((slots, LANES), jnp.float32),
            pltpu.VMEM((PB * n_row, LANES), jnp.float32),
            pltpu.VMEM((n_row - 1, PB * n_row, LANES), jnp.float32),
            pltpu.VMEM((PB * n_row, LANES), jnp.float32),
            pltpu.VMEM((PB * n_row, sets, LANES), jnp.float32),
            pltpu.VMEM((K_TERMS - 1,) + piece, jnp.bfloat16),
            pltpu.VMEM((K_TERMS - 1, n_row - 1) + piece, jnp.bfloat16),
            pltpu.VMEM((slots // 2 + 1, sets, LANES), jnp.float32),
            pltpu.VMEM((slots // 2 + 1, sets, LANES), jnp.float32),
            pltpu.VMEM((K_TERMS, n_col - 1) + piece, jnp.bfloat16),
            pltpu.VMEM((K_TERMS, n_col - 1) + piece, jnp.bfloat16),
            pltpu.VMEM((8, wide), jnp.int32),
            pltpu.SMEM((8, wide), jnp.int32),
            dma((chunks,)),
            dma,
            dma((n_row - 1,)),
            dma((n_row - 1,)),
            dma((K_TERMS - 1, n_row - 1)),
            dma((K_TERMS - 1, n_row - 1)),
            dma((K_TERMS, n_col - 1)),
            dma((K_TERMS, n_col - 1)),
        ],
        compiler_params=pltpu.CompilerParams(
            collective_id=0, has_side_effects=True, vmem_limit_bytes=60 * 1024 * 1024
        ),
        name="heat_kernel",
    )(tiles, tile_rows, tile_cols, tile_counts, seed_pages, seed_mass, heat_time)


def solution(mesh):
    in_specs = (
        P(("parts", "row"), "col", None, None, None),
        P(("parts", "row"), "col", None),
        P(("parts", "row"), "col", None),
        P(("parts", "row"), "col"),
        P("parts", None),
        P("parts", None),
        P("parts"),
    )
    out_specs = P(("parts", "row", "col"), None, None)
    return jax.shard_map(
        per_device, mesh=mesh, in_specs=in_specs, out_specs=out_specs, check_vma=False
    )
```
